768 devices in a mesh: frame: 24 (over z, x_lo), pipe: 4 (over x_hi, core), dp: 8 (over y).
Axes of the slice: x: 4 (x_hi: 2, x_lo: 2; x = x_hi * 2 + x_lo), y: 8, z: 12, core: 2. Of those that a mesh axis runs over, the one named last changes fastest.
Arguments:
- acts: bfloat16 [4, 8, 192, 24, 1280], P('pipe', 'dp', 'frame'), may hold values from -18 to 18
- cotangent: bfloat16 [4, 8, 192, 24, 1280], P('pipe', 'dp', 'frame'), may hold values from -6 to 6
- w_query: bfloat16 [4, 1280, 768], P('pipe'), may hold values from -0.15625 to 0.15625
- w_key: bfloat16 [4, 1280, 768], P('pipe'), may hold values from -0.15625 to 0.15625
- w_value: bfloat16 [4, 1280, 768], P('pipe'), may hold values from -0.15625 to 0.15625
- w_out: bfloat16 [4, 1280, 768], P('pipe'), may hold values from -0.21875 to 0.21875
Outputs:
- sent_grad: bfloat16 [4, 8, 192, 24, 1280], P('pipe', 'dp', 'frame')
- grad_value: float32 [4, 1280, 768], P('pipe', None, ('frame', 'dp'))
The draws below stay inside these ranges and needn't reach their ends.
All inputs are finite; a program needn't handle non-finite values.
Results may differ from the reference program's by a relative error of at most 0.017.
The reference program's roundings to bfloat16 on the way count: a program that leaves them out, or rounds other values in their place, can miss the bound.
Values may be sent and summed in bfloat16 or wider, within the bound.
A program may use at most 64 MiB of HBM per device.

```python
import jax
import jax.numpy as jnp
from jax import lax

C = 1280
HEADS = 12
HEAD_DIM = 64
INNER = 768
FRAMES = 192
POS = 24
CLIPS = 8
PIPE = 4


def draw_acts(key, part):
    shape = (PIPE, CLIPS, FRAMES, POS, C)
    first_key = jax.random.fold_in(key, 0)
    result = jax.random.truncated_normal(first_key, -6.0, 6.0, shape, jnp.float32)
    return result.astype(jnp.bfloat16)


def block_levels(rng, extent, cuts, smallest, high):
    def one(dim, blocks):
        steps = jax.random.uniform(jax.random.fold_in(jax.random.fold_in(rng, 6), dim), (blocks,), jnp.float32, smallest / len(cuts), high / len(cuts))
        return jnp.repeat(jnp.exp(steps), extent[dim] // blocks).reshape((-1,) + (1,) * (len(extent) - dim - 1))

    gain = one(*cuts[0])
    for cut in cuts[1:]:
        gain = gain * one(*cut)
    return gain


def bell_draw(stream_key, extent, width, reach, cuts=(), held_as=jnp.bfloat16):
    values = width * jax.random.normal(stream_key, extent, jnp.float32)
    if cuts:
        values = values * block_levels(stream_key, extent, cuts, -0.22, 0.18)
    return jnp.clip(values, -reach, reach).astype(held_as)


def setup_inputs(seed: int = 0) -> dict:
    arg_keys = jax.random.split(jax.random.key(seed), 7)
    acts = draw_acts(jax.random.fold_in(arg_keys[6], 71), 0)
    cotangent = bell_draw(arg_keys[1], (PIPE, CLIPS, FRAMES, POS, C), 1.0, 6.0, ((0, 4), (1, 8), (2, 24)))
    w_query = bell_draw(arg_keys[2], (PIPE, C, INNER), C ** -0.5, 0.15625, ((0, 4),))
    w_key = bell_draw(arg_keys[3], (PIPE, C, INNER), C ** -0.5, 0.15625, ((0, 4),))
    w_value = bell_draw(arg_keys[4], (PIPE, C, INNER), C ** -0.5, 0.15625, ((0, 4),))
    w_out = bell_draw(arg_keys[5], (PIPE, C, INNER), INNER ** -0.5, 0.21875, ((0, 4),))
    return {"acts": acts, "cotangent": cotangent, "w_query": w_query, "w_key": w_key, "w_value": w_value, "w_out": w_out}


score_scale = 0.125


def flatten_rows(array):
    return array.reshape(-1, array.shape[-1])


def attend_back(inputs, projected, w_query, w_key, w_value):
    frames = inputs.shape[0]
    places = inputs.shape[1]

    def project_heads(weight):
        result = jnp.dot(inputs, weight, preferred_element_type=jnp.float32).astype(jnp.bfloat16)
        return result.reshape(frames, places, HEADS, HEAD_DIM)

    queries = project_heads(w_query)
    key_rows = project_heads(w_key)
    values = project_heads(w_value)
    query_full = queries.astype(jnp.float32)
    key_full = key_rows.astype(jnp.float32)
    value_full = values.astype(jnp.float32)
    scores = jnp.einsum("iphd,jphd->phij", query_full, key_full) * score_scale
    probability = jax.nn.softmax(scores, axis=-1)
    prob_short = lax.optimization_barrier(probability.astype(jnp.bfloat16)).astype(jnp.float32)
    proj_full = projected.reshape(frames, places, HEADS, HEAD_DIM).astype(jnp.float32)
    grad_prob = jnp.einsum("iphd,jphd->phij", proj_full, value_full)
    value_grad = jnp.einsum("phij,iphd->jphd", prob_short, proj_full).astype(jnp.bfloat16)
    score_grad = probability * (grad_prob - jnp.sum(grad_prob * probability, axis=-1, keepdims=True))
    score_short = lax.optimization_barrier(score_grad.astype(jnp.bfloat16)).astype(jnp.float32)
    query_grad = (jnp.einsum("phij,jphd->iphd", score_short, key_full) * score_scale).astype(jnp.bfloat16)
    key_grad = (jnp.einsum("phij,iphd->jphd", score_short, query_full) * score_scale).astype(jnp.bfloat16)
    inner = HEADS * HEAD_DIM
    query_grad = query_grad.reshape(frames, places, inner)
    key_grad = key_grad.reshape(frames, places, inner)
    value_grad = value_grad.reshape(frames, places, inner)
    branch = jnp.dot(query_grad, w_query.T, preferred_element_type=jnp.float32)
    branch = branch + jnp.dot(key_grad, w_key.T, preferred_element_type=jnp.float32)
    branch = branch + jnp.dot(value_grad, w_value.T, preferred_element_type=jnp.float32)
    branch = branch.astype(jnp.bfloat16)
    weight_grad = jnp.dot(flatten_rows(inputs).T, flatten_rows(value_grad), preferred_element_type=jnp.float32)
    return branch, weight_grad


def clip_terms(inputs, upstream, w_query, w_key, w_value, w_out):
    projected = jnp.dot(upstream, w_out, preferred_element_type=jnp.float32).astype(jnp.bfloat16)
    branch, value_part = attend_back(inputs, projected, w_query, w_key, w_value)
    input_grad = (upstream.astype(jnp.float32) + branch.astype(jnp.float32)).astype(jnp.bfloat16)
    return input_grad, value_part


def reference(acts, cotangent, w_query, w_key, w_value, w_out):
    def section(packed):
        inputs, upstream, query_weight, key_weight, value_weight, out_weight = packed

        def one_clip(pair):
            return clip_terms(pair[0], pair[1], query_weight, key_weight, value_weight, out_weight)

        input_grad, value_parts = lax.map(one_clip, (inputs, upstream))
        return input_grad, jnp.sum(value_parts, axis=0)

    input_grad, grad_value = lax.map(section, (acts, cotangent, w_query, w_key, w_value, w_out))
    sent_grad = jnp.concatenate([input_grad[1:], jnp.zeros_like(input_grad[:1])], axis=0)
    return sent_grad, grad_value
```

```python
import functools

import jax
import jax.numpy as jnp
from jax import lax
from jax.experimental import pallas as pl
from jax.experimental.pallas import tpu as pltpu
from jax.sharding import PartitionSpec as P

HEADS = 12
HEAD_DIM = 64
PAIR = 2 * HEAD_DIM
PAIRS = HEADS // 2
SCALE = 0.125

BF16 = jnp.bfloat16
F32 = jnp.float32
MESH = pl.DeviceIdType.MESH

NN = (((1,), (0,)), ((), ()))
NT = (((1,), (1,)), ((), ()))
TN = (((0,), (0,)), ((), ()))


def dot(a, b, dims=NN):
    return lax.dot_general(a, b, dims, preferred_element_type=F32)


def wait_bytes(ref, sem):
    pltpu.make_async_copy(ref, ref, sem).wait()


def kernel(
    nf,
    ny,
    np_,
    acts,
    cot,
    w_query,
    w_key,
    w_value,
    w_out,
    sent,
    gvalue,
    acts_rx,
    proj_rx,
    proj_tx,
    cot_v,
    cot_rx,
    ret_tx,
    ret_rx,
    wq_v,
    wk_v,
    wv_v,
    wo_v,
    q_s,
    k_s,
    v_s,
    vg_s,
    dq_s,
    dk_s,
    order,
    vgt_b,
    prob,
    gv,
    rs_tx,
    rs_rx,
    fin_f,
    fin_tx,
    fin_rx,
    local_sem,
    acts_sem,
    proj_sem,
    cot_sem,
    ret_sem,
    fin_sem,
    rs_send,
    rs_recv,
):
    me = lax.axis_index("frame")
    pipe = lax.axis_index("pipe")
    clip = lax.axis_index("dp")
    per = acts_rx.shape[1]
    chans = acts_rx.shape[2]
    inner = proj_rx.shape[2]
    rows = nf * per
    half = chans // 2
    reach = ny // 2
    messages = 2 * reach - 1
    mine = gvalue.shape[0]
    size = mine * nf

    loads = []
    for i, (src, dst) in enumerate(
        (
            (w_out, wo_v),
            (cot, cot_v),
            (acts.at[me], acts_rx.at[0]),
            (w_query, wq_v),
            (w_key, wk_v),
            (w_value, wv_v),
        )
    ):
        load = pltpu.make_async_copy(src, dst, local_sem.at[i])
        load.start()
        loads.append(load)

    barrier = pltpu.get_barrier_semaphore()
    up = lax.rem(clip + 1, ny)
    down = lax.rem(clip + ny - 1, ny)

    def greet(k, carry):
        pl.semaphore_signal(
            barrier, inc=1, device_id={"frame": lax.rem(me + k, nf)}, device_id_type=MESH
        )
        return carry

    lax.fori_loop(1, nf, greet, 0)
    for y in (up, down):
        pl.semaphore_signal(barrier, inc=1, device_id={"dp": y}, device_id_type=MESH)
    pl.semaphore_signal(
        barrier, inc=1, device_id={"pipe": lax.rem(pipe + 1, np_)}, device_id_type=MESH
    )
    pl.semaphore_wait(barrier, nf + 2)

    def shift_of(i):
        near = lax.div(i, 2)
        odd = lax.rem(i, 2)
        return (near + 1) * (1 - odd) + (nf - 1 - near) * odd

    def spread(src_of, rx, sems):
        def one(i, carry):
            k = shift_of(i)
            to = lax.rem(me + k, nf)
            pltpu.make_async_remote_copy(
                src_ref=src_of(to),
                dst_ref=rx.at[k],
                send_sem=sems.at[0],
                recv_sem=sems.at[1],
                device_id={"frame": to},
                device_id_type=MESH,
            ).start()
            return carry

        lax.fori_loop(0, nf - 1, one, 0)

    others = pl.ds(1, nf - 1)

    spread(lambda to: acts.at[to], acts_rx, acts_sem)

    loads[0].wait()
    loads[1].wait()
    projected = dot(cot_v[...].reshape(rows, chans), wo_v[...]).astype(BF16)
    proj_tx[...] = projected.reshape(nf, per, inner)
    proj_rx[0] = proj_tx[me]
    spread(lambda to: proj_tx.at[to], proj_rx, proj_sem)

    @pl.when(pipe > 0)
    def _():
        pltpu.make_async_remote_copy(
            src_ref=cot,
            dst_ref=cot_rx,
            send_sem=cot_sem.at[0],
            recv_sem=cot_sem.at[1],
            device_id={"pipe": pipe - 1},
            device_id_type=MESH,
        ).start()

    at = lax.broadcasted_iota(jnp.int32, (inner, inner), 0)
    column = lax.rem(lax.div(at, mine), nf) * (ny * mine) + lax.div(at, size) * mine + lax.rem(at, mine)
    order[...] = jnp.where(
        column == lax.broadcasted_iota(jnp.int32, (inner, inner), 1), 1.0, 0.0
    ).astype(BF16)

    for load in loads[2:]:
        load.wait()
    wait_bytes(acts_rx.at[others], acts_sem.at[1])
    inputs = acts_rx[...].reshape(rows, chans)
    q_s[...] = dot(inputs, wq_v[...]).astype(BF16)
    k_s[...] = dot(inputs, wk_v[...]).astype(BF16)
    v_s[...] = dot(inputs, wv_v[...]).astype(BF16)
    wait_bytes(proj_rx.at[others], proj_sem.at[1])
    lane = lax.broadcasted_iota(jnp.int32, (1, PAIR), 1)
    masks = [jnp.where(lane // HEAD_DIM == e, 1.0, 0.0).astype(BF16) for e in range(2)]

    for pair in range(PAIRS):
        cols = pl.ds(pair * PAIR, PAIR)
        q = q_s[:, cols]
        k = k_s[:, cols]
        p = proj_rx[:, :, cols].reshape(rows, PAIR)
        total = jnp.zeros((rows, PAIR), F32)
        for e in range(2):
            scores = dot(k * masks[e], q, NT) * SCALE
            scores = jnp.exp(scores - jnp.max(scores, axis=0, keepdims=True))
            scores = scores * (1.0 / jnp.sum(scores, axis=0, keepdims=True))
            prob[2 * pair + e] = scores
            total = total + dot(scores.astype(BF16), p * masks[e])
        vg_s[:, cols] = total.astype(BF16)

    vgt_b[...] = dot(order[...], vg_s[...], NT).astype(BF16)
    for y in range(ny):
        gv[y] = dot(vgt_b[y * size : (y + 1) * size, :], inputs)

    def own(o, h):
        return gv[o, :, h * half : (h + 1) * half]

    def ring(d, j):
        return pltpu.make_async_remote_copy(
            src_ref=rs_tx.at[d, j],
            dst_ref=rs_rx.at[d, j],
            send_sem=rs_send.at[d, j],
            recv_sem=rs_recv.at[d, j],
            device_id={"dp": (up, down)[d]},
            device_id_type=MESH,
        )

    def ring_step(j):
        away = reach - (j + 1) // 2
        for d in range(2):
            h = (j + d) % 2
            o = lax.rem(clip + (away if d == 0 else ny - away), ny)
            value = own(o, h)
            if j >= 2:
                ring(d, j - 2).wait_recv()
                value = value + rs_rx[d, j - 2].astype(F32)
            rs_tx[d, j] = value.astype(BF16)
            ring(d, j).start()

    for j in range(min(2, messages)):
        ring_step(j)

    for pair in range(PAIRS):
        cols = pl.ds(pair * PAIR, PAIR)
        q = q_s[:, cols]
        k = k_s[:, cols]
        v = v_s[:, cols]
        p = proj_rx[:, :, cols].reshape(rows, PAIR)
        dq = jnp.zeros((rows, PAIR), F32)
        dk = jnp.zeros((rows, PAIR), F32)
        for e in range(2):
            probability = prob[2 * pair + e]
            grad = dot(v * masks[e], p, NT)
            mean = jnp.sum(grad * probability, axis=0, keepdims=True)
            grad = (probability * (grad - mean)).astype(BF16)
            dk = dk + dot(grad, q * masks[e])
            dq = dq + dot(grad, k * masks[e], TN)
        dq_s[:, cols] = (dq * SCALE).astype(BF16)
        dk_s[:, cols] = (dk * SCALE).astype(BF16)

    @pl.when(pipe > 0)
    def _():
        branch = dot(dq_s[...], wq_v[...], NT)
        branch = branch + dot(dk_s[...], wk_v[...], NT)
        branch = branch + dot(vg_s[...], wv_v[...], NT)
        ret_tx[...] = branch.astype(BF16).reshape(nf, per, chans)

        def one(k, carry):
            to = lax.rem(me - k + nf, nf)
            pltpu.make_async_remote_copy(
                src_ref=ret_tx.at[k],
                dst_ref=ret_rx.at[me],
                send_sem=ret_sem.at[0],
                recv_sem=ret_sem.at[1],
                device_id={"frame": to, "pipe": pipe - 1},
                device_id_type=MESH,
            ).start()
            return carry

        lax.fori_loop(0, nf, one, 0)

    for j in range(2, messages):
        ring_step(j)

    for d in range(2):
        for j in range(max(0, messages - 2), messages):
            ring(d, j).wait_recv()
    for h in range(2):
        value = own(clip, h)
        for d in range(2):
            j = messages - 1 - (h + d) % 2
            if j >= 0:
                value = value + rs_rx[d, j].astype(F32)
        fin_f[h] = value
    for f in range(nf):
        at = slice(f * mine, (f + 1) * mine)
        fin_tx[f] = jnp.concatenate([fin_f[0, at, :], fin_f[1, at, :]], axis=0).astype(BF16)
    fin_rx[0] = fin_tx[me]
    spread(lambda to: fin_tx.at[to], fin_rx, fin_sem)

    @pl.when(pipe < np_ - 1)
    def _():
        wait_bytes(cot_rx, cot_sem.at[1])
        wait_bytes(ret_rx, ret_sem.at[1])
        sent[...] = (cot_rx[...].astype(F32) + ret_rx[...].astype(F32)).astype(BF16)

    @pl.when(pipe == np_ - 1)
    def _():
        sent[...] = jnp.zeros_like(sent)

    wait_bytes(fin_rx.at[others], fin_sem.at[1])
    total = jnp.sum(fin_rx[...].astype(F32), axis=0)
    for h in range(2):
        gvalue[:, h * half : (h + 1) * half] = total[h * mine : (h + 1) * mine]

    wait_bytes(acts_rx.at[others], acts_sem.at[0])
    wait_bytes(proj_rx.at[others], proj_sem.at[0])
    wait_bytes(fin_rx.at[others], fin_sem.at[0])
    for d in range(2):
        for j in range(messages):
            ring(d, j).wait_send()

    @pl.when(pipe > 0)
    def _():
        wait_bytes(cot_rx, cot_sem.at[0])
        wait_bytes(ret_rx, ret_sem.at[0])


def body(nf, ny, np_, acts, cotangent, w_query, w_key, w_value, w_out):
    per, places, chans = acts.shape[2:]
    inner = w_out.shape[2]
    rows = nf * per
    mine = inner // (nf * ny)
    messages = 2 * (ny // 2) - 1
    half = chans // 2
    by_place = [jnp.swapaxes(a[0, 0], 0, 1) for a in (acts, cotangent)]
    anywhere = pl.BlockSpec(memory_space=pl.ANY)
    in_vmem = pl.BlockSpec(memory_space=pltpu.VMEM)
    sent, gvalue = pl.pallas_call(
        functools.partial(kernel, nf, ny, np_),
        out_shape=(
            jax.ShapeDtypeStruct((places, per, chans), BF16),
            jax.ShapeDtypeStruct((mine, chans), F32),
        ),
        in_specs=[anywhere] * 6,
        out_specs=(in_vmem, in_vmem),
        scratch_shapes=[
            pltpu.VMEM((nf, per, chans), BF16),
            pltpu.VMEM((nf, per, inner), BF16),
            pltpu.VMEM((nf, per, inner), BF16),
            pltpu.VMEM((nf, per, chans), BF16),
            pltpu.VMEM((nf, per, chans), BF16),
            pltpu.VMEM((nf, per, chans), BF16),
            pltpu.VMEM((nf, per, chans), BF16),
            pltpu.VMEM((chans, inner), BF16),
            pltpu.VMEM((chans, inner), BF16),
            pltpu.VMEM((chans, inner), BF16),
            pltpu.VMEM((chans, inner), BF16),
            pltpu.VMEM((rows, inner), BF16),
            pltpu.VMEM((rows, inner), BF16),
            pltpu.VMEM((rows, inner), BF16),
            pltpu.VMEM((rows, inner), BF16),
            pltpu.VMEM((rows, inner), BF16),
            pltpu.VMEM((rows, inner), BF16),
            pltpu.VMEM((inner, inner), BF16),
            pltpu.VMEM((inner, rows), BF16),
            pltpu.VMEM((HEADS, rows, rows), F32),
            pltpu.VMEM((ny, mine * nf, chans), F32),
            pltpu.VMEM((2, messages, mine * nf, half), BF16),
            pltpu.VMEM((2, messages, mine * nf, half), BF16),
            pltpu.VMEM((2, mine * nf, half), F32),
            pltpu.VMEM((nf, 2 * mine, half), BF16),
            pltpu.VMEM((nf, 2 * mine, half), BF16),
            pltpu.SemaphoreType.DMA((6,)),
            pltpu.SemaphoreType.DMA((2,)),
            pltpu.SemaphoreType.DMA((2,)),
            pltpu.SemaphoreType.DMA((2,)),
            pltpu.SemaphoreType.DMA((2,)),
            pltpu.SemaphoreType.DMA((2,)),
            pltpu.SemaphoreType.DMA((2, messages)),
            pltpu.SemaphoreType.DMA((2, messages)),
        ],
        compiler_params=pltpu.CompilerParams(
            collective_id=0, has_side_effects=True, vmem_limit_bytes=56 * 1024 * 1024
        ),
        name="attention_backward",
    )(*by_place, w_query[0], w_key[0], w_value[0], w_out[0])
    return jnp.swapaxes(sent, 0, 1)[None, None], gvalue.T[None]


def solution(mesh):
    sizes = [mesh.shape[a] for a in ("frame", "dp", "pipe")]
    spread = P("pipe", "dp", "frame", None, None)
    return jax.shard_map(
        functools.partial(body, *sizes),
        mesh=mesh,
        in_specs=(spread, spread) + (P("pipe", None, None),) * 4,
        out_specs=(spread, P("pipe", None, ("frame", "dp"))),
        check_vma=False,
    )
```

```python
import functools

import jax
import jax.numpy as jnp
from jax import lax
from jax.experimental import pallas as pl
from jax.experimental.pallas import tpu as pltpu
from jax.sharding import PartitionSpec as P

HEADS = 12
HEAD_DIM = 64
PAIR = 2 * HEAD_DIM
PAIRS = HEADS // 2
SCALE = 0.125

BF16 = jnp.bfloat16
F32 = jnp.float32
MESH = pl.DeviceIdType.MESH

NN = (((1,), (0,)), ((), ()))
NT = (((1,), (1,)), ((), ()))
TN = (((0,), (0,)), ((), ()))


def dot(a, b, dims=NN):
    return lax.dot_general(a, b, dims, preferred_element_type=F32)


def wait_bytes(ref, sem):
    pltpu.make_async_copy(ref, ref, sem).wait()


def kernel(
    nf,
    ny,
    np_,
    acts,
    cot,
    w_query,
    w_key,
    w_value,
    w_out,
    sent,
    gvalue,
    acts_rx,
    proj_rx,
    proj_tx,
    acts_v,
    acts_tx,
    turn,
    cot_v,
    cot_rx,
    ret_tx,
    ret_rx,
    wq_v,
    wk_v,
    wv_v,
    wo_v,
    q_s,
    k_s,
    v_s,
    vg_s,
    dq_s,
    dk_s,
    order,
    vgt_b,
    prob,
    gv,
    rs_tx,
    rs_rx,
    fin_f,
    fin_tx,
    fin_rx,
    local_sem,
    acts_sem,
    proj_sem,
    cot_sem,
    ret_sem,
    fin_sem,
    rs_send,
    rs_recv,
    ready,
    turn_over,
):
    me = lax.axis_index("frame")
    pipe = lax.axis_index("pipe")
    clip = lax.axis_index("dp")
    per = acts_rx.shape[1]
    chans = acts_rx.shape[2]
    inner = proj_rx.shape[2]
    rows = nf * per
    half = chans // 2
    reach = ny // 2
    messages = 2 * reach - 1
    mine = gvalue.shape[0]
    size = mine * nf

    loads = []
    for i, (src, dst) in enumerate(
        (
            (acts, acts_v),
            (cot, cot_v),
            (w_out, wo_v),
            (w_query, wq_v),
            (w_key, wk_v),
            (w_value, wv_v),
        )
    ):
        load = pltpu.make_async_copy(src, dst, local_sem.at[i])
        load.start()
        loads.append(load)

    barrier = pltpu.get_barrier_semaphore()
    up = lax.rem(clip + 1, ny)
    down = lax.rem(clip + ny - 1, ny)
    second = lax.rem(pipe, 2)
    partner = pipe + 1 - 2 * second

    def greet(b, carry):
        pl.semaphore_signal(barrier, inc=1, device_id={"frame": b}, device_id_type=MESH)
        return carry

    lax.fori_loop(me + 1, nf, greet, 0)
    for y in (up, down):
        pl.semaphore_signal(barrier, inc=1, device_id={"dp": y}, device_id_type=MESH)
    for p in (lax.rem(pipe + 1, np_), partner):
        pl.semaphore_signal(barrier, inc=1, device_id={"pipe": p}, device_id_type=MESH)
    pl.semaphore_wait(barrier, me + 4)

    def answer(a, carry):
        pl.semaphore_signal(ready.at[me], inc=1, device_id={"frame": a}, device_id_type=MESH)
        return carry

    lax.fori_loop(0, me, answer, 0)

    def shift_of(i):
        near = lax.div(i, 2)
        odd = lax.rem(i, 2)
        return (near + 1) * (1 - odd) + (nf - 1 - near) * odd

    late = lax.div(2 * me, nf)

    def send(tx, rx, sends, recvs, to):
        pltpu.make_async_remote_copy(
            src_ref=tx.at[to],
            dst_ref=rx.at[me],
            send_sem=sends,
            recv_sem=recvs,
            device_id={"frame": to},
            device_id_type=MESH,
        ).start()

    def send_acts(to):
        send(acts_tx, acts_rx, acts_sem.at[2], acts_sem.at[late], to)

    def send_proj(to):
        send(proj_tx, proj_rx, proj_sem.at[0], proj_sem.at[1], to)

    def send_fin(to):
        send(fin_tx, fin_rx, fin_sem.at[0], fin_sem.at[1], to)

    def keep(tx, rx, sem):
        pltpu.make_async_copy(tx.at[me], rx.at[me], sem).start()

    def to_earlier(one):
        def step(i, carry):
            to = lax.rem(me + shift_of(i), nf)
            pl.when(to < me)(lambda: one(to))
            return carry

        lax.fori_loop(0, nf - 1, step, 0)

    others = pl.ds(1, nf - 1)

    at = lax.broadcasted_iota(jnp.int32, (rows, rows), 0)
    column = lax.rem(at, per) * nf + lax.div(at, per)
    turn[...] = jnp.where(
        column == lax.broadcasted_iota(jnp.int32, (rows, rows), 1), 1.0, 0.0
    ).astype(BF16)
    loads[0].wait()
    acts_tx[...] = dot(turn[...], acts_v[...]).astype(BF16).reshape(nf, per, chans)
    keep(acts_tx, acts_rx, acts_sem.at[late])

    to_earlier(send_acts)

    loads[1].wait()
    loads[2].wait()
    projected = dot(cot_v[...], wo_v[...]).astype(BF16)
    proj_tx[...] = dot(turn[...], projected).astype(BF16).reshape(nf, per, inner)
    keep(proj_tx, proj_rx, proj_sem.at[1])


    to_earlier(send_proj)

    def to_later(to, carry):
        pl.semaphore_wait(ready.at[to], 1)
        send_acts(to)
        send_proj(to)
        return carry

    lax.fori_loop(me + 1, nf, to_later, 0)

    @pl.when(pipe > 0)
    def _():
        pltpu.make_async_remote_copy(
            src_ref=cot_v,
            dst_ref=cot_rx,
            send_sem=cot_sem.at[0],
            recv_sem=cot_sem.at[1],
            device_id={"pipe": pipe - 1},
            device_id_type=MESH,
        ).start()

    at = lax.broadcasted_iota(jnp.int32, (inner, inner), 0)
    column = lax.rem(lax.div(at, mine), nf) * (ny * mine) + lax.div(at, size) * mine + lax.rem(at, mine)
    order[...] = jnp.where(
        column == lax.broadcasted_iota(jnp.int32, (inner, inner), 1), 1.0, 0.0
    ).astype(BF16)

    wait_bytes(acts_rx.at[others], acts_sem.at[2])
    wait_bytes(proj_rx.at[others], proj_sem.at[0])

    for load in loads[3:]:
        load.wait()
    few = nf // 2
    for e in range(2):
        slots = pl.ds(e * few, few)
        block = pl.ds(e * few * per, few * per)
        wait_bytes(acts_rx.at[slots], acts_sem.at[e])
        inputs = acts_rx[slots].reshape(few * per, chans)
        q_s[block, :] = dot(inputs, wq_v[...]).astype(BF16)
        k_s[block, :] = dot(inputs, wk_v[...]).astype(BF16)
        v_s[block, :] = dot(inputs, wv_v[...]).astype(BF16)
    inputs = acts_rx[...].reshape(rows, chans)
    wait_bytes(proj_rx, proj_sem.at[1])
    lane = lax.broadcasted_iota(jnp.int32, (1, PAIR), 1)
    masks = [jnp.where(lane // HEAD_DIM == e, 1.0, 0.0).astype(BF16) for e in range(2)]

    for pair in range(PAIRS):
        cols = pl.ds(pair * PAIR, PAIR)
        q = q_s[:, cols]
        k = k_s[:, cols]
        p = proj_rx[:, :, cols].reshape(rows, PAIR)
        total = jnp.zeros((rows, PAIR), F32)
        for e in range(2):
            scores = dot(k * masks[e], q, NT) * SCALE
            scores = jnp.exp(scores - jnp.max(scores, axis=0, keepdims=True))
            scores = scores * (1.0 / jnp.sum(scores, axis=0, keepdims=True))
            prob[2 * pair + e] = scores
            total = total + dot(scores.astype(BF16), p * masks[e])
        vg_s[:, cols] = total.astype(BF16)

    vgt_b[...] = dot(order[...], vg_s[...], NT).astype(BF16)

    def sum_for(away):
        o = lax.rem(clip + away, ny)
        at = pl.ds(pl.multiple_of(o * size, size), size)
        gv[o] = dot(vgt_b[at, :], inputs)

    def own(o, h):
        return gv[o, :, h * half : (h + 1) * half]

    def ring(d, j):
        return pltpu.make_async_remote_copy(
            src_ref=rs_tx.at[d, j],
            dst_ref=rs_rx.at[d, j],
            send_sem=rs_send.at[d, j],
            recv_sem=rs_recv.at[d, j],
            device_id={"dp": (up, down)[d]},
            device_id_type=MESH,
        )

    def ring_step(j):
        away = reach - (j + 1) // 2
        for d in range(2):
            h = (j + d) % 2
            o = lax.rem(clip + (away if d == 0 else ny - away), ny)
            value = own(o, h)
            if j >= 2:
                ring(d, j - 2).wait_recv()
                value = value + rs_rx[d, j - 2].astype(F32)
            rs_tx[d, j] = value.astype(BF16)
            ring(d, j).start()

    sum_for(reach)
    ring_step(0)
    if messages > 1:
        sum_for(reach - 1)
        sum_for(ny - reach + 1)
        ring_step(1)
    for away in range(reach - 1):
        sum_for(away)
        if away:
            sum_for(ny - away)
    if messages == 1:
        sum_for(0)

    for pair in range(PAIRS):
        cols = pl.ds(pair * PAIR, PAIR)
        q = q_s[:, cols]
        k = k_s[:, cols]
        v = v_s[:, cols]
        p = proj_rx[:, :, cols].reshape(rows, PAIR)
        dq = jnp.zeros((rows, PAIR), F32)
        dk = jnp.zeros((rows, PAIR), F32)
        for e in range(2):
            probability = prob[2 * pair + e]
            grad = dot(v * masks[e], p, NT)
            mean = jnp.sum(grad * probability, axis=0, keepdims=True)
            grad = (probability * (grad - mean)).astype(BF16)
            dk = dk + dot(grad, q * masks[e])
            dq = dq + dot(grad, k * masks[e], TN)
        dq_s[:, cols] = (dq * SCALE).astype(BF16)
        dk_s[:, cols] = (dk * SCALE).astype(BF16)

    if messages > 2:
        ring_step(2)

    @pl.when(pipe > 0)
    def _():
        branch = dot(dq_s[...], wq_v[...], NT)
        branch = branch + dot(dk_s[...], wk_v[...], NT)
        branch = branch + dot(vg_s[...], wv_v[...], NT)
        ret_tx[...] = branch.astype(BF16).reshape(nf, per, chans)

        def one(i, carry):
            to = lax.rem(me + shift_of(i) * jnp.minimum(nf - 1 - i, 1), nf)
            pltpu.make_async_remote_copy(
                src_ref=ret_tx.at[to],
                dst_ref=ret_rx.at[me],
                send_sem=ret_sem.at[0],
                recv_sem=ret_sem.at[1],
                device_id={"frame": to, "pipe": pipe - 1},
                device_id_type=MESH,
            ).start()
            return carry

        lax.fori_loop(0, nf, one, 0)

    for j in range(3, messages):
        ring_step(j)

    for d in range(2):
        for j in range(max(0, messages - 2), messages):
            ring(d, j).wait_recv()
    for h in range(2):
        value = own(clip, h)
        for d in range(2):
            j = messages - 1 - (h + d) % 2
            if j >= 0:
                value = value + rs_rx[d, j].astype(F32)
        fin_f[h] = value
    for f in range(nf):
        at = slice(f * mine, (f + 1) * mine)
        fin_tx[f] = jnp.concatenate([fin_f[0, at, :], fin_f[1, at, :]], axis=0).astype(BF16)
    keep(fin_tx, fin_rx, fin_sem.at[1])

    def finish(i, carry):
        send_fin(lax.rem(me + shift_of(i), nf))
        return carry

    lax.fori_loop(0, nf - 1, finish, 0)

    @pl.when(pipe < np_ - 1)
    def _():
        wait_bytes(cot_rx, cot_sem.at[1])
        wait_bytes(ret_rx, ret_sem.at[1])
        branch = dot(turn[...], ret_rx[...].reshape(rows, chans), TN)
        sent[...] = (cot_rx[...].astype(F32) + branch).astype(BF16)

    @pl.when(pipe == np_ - 1)
    def _():
        sent[...] = jnp.zeros_like(sent)

    wait_bytes(fin_rx, fin_sem.at[1])
    total = jnp.sum(fin_rx[...].astype(F32), axis=0)
    for h in range(2):
        gvalue[:, h * half : (h + 1) * half] = total[h * mine : (h + 1) * mine]

    wait_bytes(fin_rx.at[others], fin_sem.at[0])
    for d in range(2):
        for j in range(messages):
            ring(d, j).wait_send()

    @pl.when(pipe > 0)
    def _():
        wait_bytes(cot_rx, cot_sem.at[0])
        wait_bytes(ret_rx, ret_sem.at[0])


def body(nf, ny, np_, acts, cotangent, w_query, w_key, w_value, w_out):
    per, places, chans = acts.shape[2:]
    inner = w_out.shape[2]
    rows = nf * per
    mine = inner // (nf * ny)
    messages = 2 * (ny // 2) - 1
    half = chans // 2
    flat = [a[0, 0].reshape(per * places, chans) for a in (acts, cotangent)]
    anywhere = pl.BlockSpec(memory_space=pl.ANY)
    in_vmem = pl.BlockSpec(memory_space=pltpu.VMEM)
    sent, gvalue = pl.pallas_call(
        functools.partial(kernel, nf, ny, np_),
        out_shape=(
            jax.ShapeDtypeStruct((rows, chans), BF16),
            jax.ShapeDtypeStruct((mine, chans), F32),
        ),
        in_specs=[anywhere] * 6,
        out_specs=(in_vmem, in_vmem),
        scratch_shapes=[
            pltpu.VMEM((nf, per, chans), BF16),
            pltpu.VMEM((nf, per, inner), BF16),
            pltpu.VMEM((nf, per, inner), BF16),
            pltpu.VMEM((rows, chans), BF16),
            pltpu.VMEM((nf, per, chans), BF16),
            pltpu.VMEM((rows, rows), BF16),
            pltpu.VMEM((rows, chans), BF16),
            pltpu.VMEM((rows, chans), BF16),
            pltpu.VMEM((nf, per, chans), BF16),
            pltpu.VMEM((nf, per, chans), BF16),
            pltpu.VMEM((chans, inner), BF16),
            pltpu.VMEM((chans, inner), BF16),
            pltpu.VMEM((chans, inner), BF16),
            pltpu.VMEM((chans, inner), BF16),
            pltpu.VMEM((rows, inner), BF16),
            pltpu.VMEM((rows, inner), BF16),
            pltpu.VMEM((rows, inner), BF16),
            pltpu.VMEM((rows, inner), BF16),
            pltpu.VMEM((rows, inner), BF16),
            pltpu.VMEM((rows, inner), BF16),
            pltpu.VMEM((inner, inner), BF16),
            pltpu.VMEM((inner, rows), BF16),
            pltpu.VMEM((HEADS, rows, rows), F32),
            pltpu.VMEM((ny, mine * nf, chans), F32),
            pltpu.VMEM((2, messages, mine * nf, half), BF16),
            pltpu.VMEM((2, messages, mine * nf, half), BF16),
            pltpu.VMEM((2, mine * nf, half), F32),
            pltpu.VMEM((nf, 2 * mine, half), BF16),
            pltpu.VMEM((nf, 2 * mine, half), BF16),
            pltpu.SemaphoreType.DMA((6,)),
            pltpu.SemaphoreType.DMA((3,)),
            pltpu.SemaphoreType.DMA((2,)),
            pltpu.SemaphoreType.DMA((2,)),
            pltpu.SemaphoreType.DMA((2,)),
            pltpu.SemaphoreType.DMA((2,)),
            pltpu.SemaphoreType.DMA((2, messages)),
            pltpu.SemaphoreType.DMA((2, messages)),
            pltpu.SemaphoreType.REGULAR((nf,)),
            pltpu.SemaphoreType.REGULAR,
        ],
        compiler_params=pltpu.CompilerParams(
            collective_id=0, has_side_effects=True, vmem_limit_bytes=56 * 1024 * 1024
        ),
        name="attention_backward",
    )(*flat, w_query[0], w_key[0], w_value[0], w_out[0])
    return sent.reshape(1, 1, per, places, chans), gvalue.T[None]


def solution(mesh):
    sizes = [mesh.shape[a] for a in ("frame", "dp", "pipe")]
    spread = P("pipe", "dp", "frame", None, None)
    return jax.shard_map(
        functools.partial(body, *sizes),
        mesh=mesh,
        in_specs=(spread, spread) + (P("pipe", None, None),) * 4,
        out_specs=(spread, P("pipe", None, ("frame", "dp"))),
        check_vma=False,
    )
```

```python
import functools

import jax
import jax.numpy as jnp
from jax import lax
from jax.experimental import pallas as pl
from jax.experimental.pallas import tpu as pltpu
from jax.sharding import PartitionSpec as P

HEADS = 12
HEAD_DIM = 64
PAIR = 2 * HEAD_DIM
PAIRS = HEADS // 2
SCALE = 0.125

BF16 = jnp.bfloat16
F32 = jnp.float32
MESH = pl.DeviceIdType.MESH

NN = (((1,), (0,)), ((), ()))
NT = (((1,), (1,)), ((), ()))
TN = (((0,), (0,)), ((), ()))


def dot(a, b, dims=NN):
    return lax.dot_general(a, b, dims, preferred_element_type=F32)


def wait_bytes(ref, sem):
    pltpu.make_async_copy(ref, ref, sem).wait()


def kernel(
    nf,
    ny,
    np_,
    acts,
    cot,
    w_query,
    w_key,
    w_value,
    w_out,
    sent,
    gvalue,
    acts_rx,
    proj_rx,
    proj_tx,
    acts_v,
    acts_tx,
    turn,
    cot_v,
    cot_rx,
    ret_tx,
    ret_rx,
    wq_v,
    wk_v,
    wv_v,
    wo_v,
    q_s,
    k_s,
    v_s,
    vg_s,
    dq_s,
    dk_s,
    order,
    vgt_b,
    prob,
    gv,
    px_tx,
    px_rx,
    rs_tx,
    rs_rx,
    fin_f,
    fin_tx,
    fin_rx,
    local_sem,
    acts_sem,
    proj_sem,
    cot_sem,
    ret_sem,
    fin_sem,
    rs_send,
    rs_recv,
    px_send,
    px_recv,
    ready,
):
    me = lax.axis_index("frame")
    pipe = lax.axis_index("pipe")
    clip = lax.axis_index("dp")
    per = acts_rx.shape[1]
    chans = acts_rx.shape[2]
    inner = proj_rx.shape[2]
    rows = nf * per
    half = chans // 2
    reach = ny // 2
    mine = gvalue.shape[0]
    size = mine * nf
    part = size // 2
    side = lax.rem(me, 2)
    beside = me + 1 - 2 * side

    loads = []
    for i, (src, dst) in enumerate(
        (
            (acts, acts_v),
            (cot, cot_v),
            (w_out, wo_v),
            (w_query, wq_v),
            (w_key, wk_v),
            (w_value, wv_v),
        )
    ):
        load = pltpu.make_async_copy(src, dst, local_sem.at[i])
        load.start()
        loads.append(load)

    barrier = pltpu.get_barrier_semaphore()
    up = lax.rem(clip + 1, ny)
    down = lax.rem(clip + ny - 1, ny)

    def greet(b, carry):
        pl.semaphore_signal(barrier, inc=1, device_id={"frame": b}, device_id_type=MESH)
        return carry

    lax.fori_loop(me + 1, nf, greet, 0)
    for y in (up, down):
        pl.semaphore_signal(barrier, inc=1, device_id={"dp": y}, device_id_type=MESH)
    pl.semaphore_signal(
        barrier, inc=1, device_id={"pipe": lax.rem(pipe + 1, np_)}, device_id_type=MESH
    )
    pl.semaphore_wait(barrier, me + 3)

    def answer(a, carry):
        pl.semaphore_signal(ready.at[me], inc=1, device_id={"frame": a}, device_id_type=MESH)
        return carry

    lax.fori_loop(0, me, answer, 0)

    def shift_of(i):
        near = lax.div(i, 2)
        odd = lax.rem(i, 2)
        return (near + 1) * (1 - odd) + (nf - 1 - near) * odd

    late = lax.div(2 * me, nf)

    def send(tx, rx, sends, recvs, to):
        pltpu.make_async_remote_copy(
            src_ref=tx.at[to],
            dst_ref=rx.at[me],
            send_sem=sends,
            recv_sem=recvs,
            device_id={"frame": to},
            device_id_type=MESH,
        ).start()

    def send_acts(to):
        send(acts_tx, acts_rx, acts_sem.at[2], acts_sem.at[late], to)

    def send_proj(to):
        send(proj_tx, proj_rx, proj_sem.at[0], proj_sem.at[1], to)

    def send_fin(to):
        send(fin_tx, fin_rx, fin_sem.at[0], fin_sem.at[1], to)

    def keep(tx, rx, sem):
        pltpu.make_async_copy(tx.at[me], rx.at[me], sem).start()

    def to_earlier(one):
        def step(i, carry):
            to = lax.rem(me + shift_of(i), nf)
            pl.when(to < me)(lambda: one(to))
            return carry

        lax.fori_loop(0, nf - 1, step, 0)

    others = pl.ds(1, nf - 1)

    at = lax.broadcasted_iota(jnp.int32, (rows, rows), 0)
    column = lax.rem(at, per) * nf + lax.div(at, per)
    turn[...] = jnp.where(
        column == lax.broadcasted_iota(jnp.int32, (rows, rows), 1), 1.0, 0.0
    ).astype(BF16)
    loads[0].wait()
    acts_tx[...] = dot(turn[...], acts_v[...]).astype(BF16).reshape(nf, per, chans)
    keep(acts_tx, acts_rx, acts_sem.at[late])

    to_earlier(send_acts)

    loads[1].wait()
    loads[2].wait()
    projected = dot(cot_v[...], wo_v[...]).astype(BF16)
    proj_tx[...] = dot(turn[...], projected).astype(BF16).reshape(nf, per, inner)
    keep(proj_tx, proj_rx, proj_sem.at[1])
    to_earlier(send_proj)

    def to_later(to, carry):
        pl.semaphore_wait(ready.at[to], 1)
        send_acts(to)
        send_proj(to)
        return carry

    lax.fori_loop(me + 1, nf, to_later, 0)

    @pl.when(pipe > 0)
    def _():
        pltpu.make_async_remote_copy(
            src_ref=cot_v,
            dst_ref=cot_rx,
            send_sem=cot_sem.at[0],
            recv_sem=cot_sem.at[1],
            device_id={"pipe": pipe - 1},
            device_id_type=MESH,
        ).start()

    at = lax.broadcasted_iota(jnp.int32, (inner, inner), 0)
    group = lax.rem(lax.div(at, mine), nf)
    frame = 2 * lax.rem(group, nf // 2) + lax.div(group, nf // 2)
    column = frame * (ny * mine) + lax.div(at, size) * mine + lax.rem(at, mine)
    order[...] = jnp.where(
        column == lax.broadcasted_iota(jnp.int32, (inner, inner), 1), 1.0, 0.0
    ).astype(BF16)

    wait_bytes(acts_rx.at[others], acts_sem.at[2])
    wait_bytes(proj_rx.at[others], proj_sem.at[0])

    for load in loads[3:]:
        load.wait()
    few = nf // 2
    for e in range(2):
        slots = pl.ds(e * few, few)
        block = pl.ds(e * few * per, few * per)
        wait_bytes(acts_rx.at[slots], acts_sem.at[e])
        inputs = acts_rx[slots].reshape(few * per, chans)
        q_s[block, :] = dot(inputs, wq_v[...]).astype(BF16)
        k_s[block, :] = dot(inputs, wk_v[...]).astype(BF16)
        v_s[block, :] = dot(inputs, wv_v[...]).astype(BF16)
    inputs = acts_rx[...].reshape(rows, chans)
    wait_bytes(proj_rx, proj_sem.at[1])
    lane = lax.broadcasted_iota(jnp.int32, (1, PAIR), 1)
    masks = [jnp.where(lane // HEAD_DIM == e, 1.0, 0.0).astype(BF16) for e in range(2)]

    for pair in range(PAIRS):
        cols = pl.ds(pair * PAIR, PAIR)
        q = q_s[:, cols]
        k = k_s[:, cols]
        p = proj_rx[:, :, cols].reshape(rows, PAIR)
        total = jnp.zeros((rows, PAIR), F32)
        for e in range(2):
            scores = dot(k * masks[e], q, NT) * SCALE
            scores = jnp.exp(scores - jnp.max(scores, axis=0, keepdims=True))
            scores = scores * (1.0 / jnp.sum(scores, axis=0, keepdims=True))
            prob[2 * pair + e] = scores
            total = total + dot(scores.astype(BF16), p * masks[e])
        vg_s[:, cols] = total.astype(BF16)

    vgt_b[...] = dot(order[...], vg_s[...], NT).astype(BF16)

    def sum_for(away):
        o = lax.rem(clip + away, ny)
        at = pl.ds(pl.multiple_of(o * size, size), size)
        gv[o] = dot(vgt_b[at, :], inputs)

    def beside_copy(t):
        return pltpu.make_async_remote_copy(
            src_ref=px_tx.at[t],
            dst_ref=px_rx.at[t],
            send_sem=px_send.at[t],
            recv_sem=px_recv.at[t],
            device_id={"frame": beside},
            device_id_type=MESH,
        )

    def turn_of(d, away):
        if away == 0:
            return ny - 1
        return 0 if away == reach else 2 * (reach - away) - 1 + d

    def swap_sides(d, away):
        t = turn_of(d, away)
        away = away if d == 0 else ny - away
        sum_for(away)
        o = lax.rem(clip + away, ny)
        at = pl.ds(pl.multiple_of((1 - side) * part, part), part)
        px_tx[t] = gv[o, at, :half].astype(BF16)
        beside_copy(t).start()

    def own(d, q, away):
        o = lax.rem(clip + (away if d == 0 else ny - away), ny)
        if q == 0:
            t = turn_of(d, away)
            beside_copy(t).wait_recv()
            at = pl.ds(pl.multiple_of(side * part, part), part)
            return gv[o, at, :half] + px_rx[t].astype(F32)
        return gv[o, (q - 1) * part : q * part, half:]

    far = ((reach, reach, reach - 1), (reach - 1, reach - 1, reach))

    def ring(d, q, away):
        return pltpu.make_async_remote_copy(
            src_ref=rs_tx.at[d, q, away - 1],
            dst_ref=rs_rx.at[d, q, away - 1],
            send_sem=rs_send.at[d, q, away - 1],
            recv_sem=rs_recv.at[d, q, away - 1],
            device_id={"dp": (up, down)[d]},
            device_id_type=MESH,
        )

    def pass_on(d, q, away):
        value = own(d, q, away)
        if away < far[d][q]:
            ring(d, q, away + 1).wait_recv()
            value = value + rs_rx[d, q, away].astype(F32)
        rs_tx[d, q, away - 1] = value.astype(BF16)
        ring(d, q, away).start()

    def long_ways(away):
        for d, q in ((1, 2), (0, 1), (0, 0)):
            pass_on(d, q, away)

    def short_ways(away):
        for d, q in ((0, 2), (1, 1), (1, 0)):
            pass_on(d, q, away)

    swap_sides(0, reach)
    pass_on(1, 2, reach)
    pass_on(0, 1, reach)
    if reach > 1:
        swap_sides(0, reach - 1)
        swap_sides(1, reach - 1)
        pass_on(0, 2, reach - 1)
        pass_on(1, 1, reach - 1)
    for away in range(reach - 2, 0, -1):
        swap_sides(0, away)
        swap_sides(1, away)
    swap_sides(0, 0)
    pass_on(0, 0, reach)
    if reach > 1:
        pass_on(1, 0, reach - 1)

    for pair in range(PAIRS):
        cols = pl.ds(pair * PAIR, PAIR)
        q = q_s[:, cols]
        k = k_s[:, cols]
        v = v_s[:, cols]
        p = proj_rx[:, :, cols].reshape(rows, PAIR)
        dq = jnp.zeros((rows, PAIR), F32)
        dk = jnp.zeros((rows, PAIR), F32)
        for e in range(2):
            probability = prob[2 * pair + e]
            grad = dot(v * masks[e], p, NT)
            mean = jnp.sum(grad * probability, axis=0, keepdims=True)
            grad = (probability * (grad - mean)).astype(BF16)
            dk = dk + dot(grad, q * masks[e])
            dq = dq + dot(grad, k * masks[e], TN)
        dq_s[:, cols] = (dq * SCALE).astype(BF16)
        dk_s[:, cols] = (dk * SCALE).astype(BF16)

    @pl.when(pipe > 0)
    def _():
        branch = dot(dq_s[...], wq_v[...], NT)
        branch = branch + dot(dk_s[...], wk_v[...], NT)
        branch = branch + dot(vg_s[...], wv_v[...], NT)
        ret_tx[...] = branch.astype(BF16).reshape(nf, per, chans)

        def one(i, carry):
            to = lax.rem(me + shift_of(i) * jnp.minimum(nf - 1 - i, 1), nf)
            pltpu.make_async_remote_copy(
                src_ref=ret_tx.at[to],
                dst_ref=ret_rx.at[me],
                send_sem=ret_sem.at[0],
                recv_sem=ret_sem.at[1],
                device_id={"frame": to, "pipe": pipe - 1},
                device_id_type=MESH,
            ).start()
            return carry

        lax.fori_loop(0, nf, one, 0)

    for away in range(reach - 1, 0, -1):
        long_ways(away)
        if away > 1:
            short_ways(away - 1)

    for q in (1, 2, 0):
        value = own(0, q, 0)
        for d in range(2):
            if far[d][q] > 0:
                ring(d, q, 1).wait_recv()
                value = value + rs_rx[d, q, 0].astype(F32)
        fin_f[q] = value
    zero = jnp.zeros((mine, half), F32)
    for f in range(nf):
        at = slice((f // 2) * mine, (f // 2 + 1) * mine)
        first = jnp.where(side == f % 2, fin_f[0, at, :], zero)
        fin_tx[f] = jnp.concatenate([first, fin_f[1 + f % 2, at, :]], axis=0).astype(BF16)
    keep(fin_tx, fin_rx, fin_sem.at[1])

    def finish(i, carry):
        send_fin(lax.rem(me + shift_of(i), nf))
        return carry

    lax.fori_loop(0, nf - 1, finish, 0)

    @pl.when(pipe < np_ - 1)
    def _():
        wait_bytes(cot_rx, cot_sem.at[1])
        wait_bytes(ret_rx, ret_sem.at[1])
        branch = dot(turn[...], ret_rx[...].reshape(rows, chans), TN)
        sent[...] = (cot_rx[...].astype(F32) + branch).astype(BF16)

    @pl.when(pipe == np_ - 1)
    def _():
        sent[...] = jnp.zeros_like(sent)

    wait_bytes(fin_rx, fin_sem.at[1])
    total = jnp.sum(fin_rx[...].astype(F32), axis=0)
    for h in range(2):
        gvalue[:, h * half : (h + 1) * half] = total[h * mine : (h + 1) * mine]

    wait_bytes(fin_rx.at[others], fin_sem.at[0])
    for t in range(ny):
        beside_copy(t).wait_send()
    for d in range(2):
        for q in range(3):
            for away in range(far[d][q], 0, -1):
                ring(d, q, away).wait_send()

    @pl.when(pipe > 0)
    def _():
        wait_bytes(cot_rx, cot_sem.at[0])
        wait_bytes(ret_rx, ret_sem.at[0])


def body(nf, ny, np_, acts, cotangent, w_query, w_key, w_value, w_out):
    per, places, chans = acts.shape[2:]
    inner = w_out.shape[2]
    rows = nf * per
    mine = inner // (nf * ny)
    reach = ny // 2
    half = chans // 2
    flat = [a[0, 0].reshape(per * places, chans) for a in (acts, cotangent)]
    anywhere = pl.BlockSpec(memory_space=pl.ANY)
    in_vmem = pl.BlockSpec(memory_space=pltpu.VMEM)
    sent, gvalue = pl.pallas_call(
        functools.partial(kernel, nf, ny, np_),
        out_shape=(
            jax.ShapeDtypeStruct((rows, chans), BF16),
            jax.ShapeDtypeStruct((mine, chans), F32),
        ),
        in_specs=[anywhere] * 6,
        out_specs=(in_vmem, in_vmem),
        scratch_shapes=[
            pltpu.VMEM((nf, per, chans), BF16),
            pltpu.VMEM((nf, per, inner), BF16),
            pltpu.VMEM((nf, per, inner), BF16),
            pltpu.VMEM((rows, chans), BF16),
            pltpu.VMEM((nf, per, chans), BF16),
            pltpu.VMEM((rows, rows), BF16),
            pltpu.VMEM((rows, chans), BF16),
            pltpu.VMEM((rows, chans), BF16),
            pltpu.VMEM((nf, per, chans), BF16),
            pltpu.VMEM((nf, per, chans), BF16),
            pltpu.VMEM((chans, inner), BF16),
            pltpu.VMEM((chans, inner), BF16),
            pltpu.VMEM((chans, inner), BF16),
            pltpu.VMEM((chans, inner), BF16),
            pltpu.VMEM((rows, inner), BF16),
            pltpu.VMEM((rows, inner), BF16),
            pltpu.VMEM((rows, inner), BF16),
            pltpu.VMEM((rows, inner), BF16),
            pltpu.VMEM((rows, inner), BF16),
            pltpu.VMEM((rows, inner), BF16),
            pltpu.VMEM((inner, inner), BF16),
            pltpu.VMEM((inner, rows), BF16),
            pltpu.VMEM((HEADS, rows, rows), F32),
            pltpu.VMEM((ny, mine * nf, chans), F32),
            pltpu.VMEM((ny, mine * nf // 2, half), BF16),
            pltpu.VMEM((ny, mine * nf // 2, half), BF16),
            pltpu.VMEM((2, 3, reach, mine * nf // 2, half), BF16),
            pltpu.VMEM((2, 3, reach, mine * nf // 2, half), BF16),
            pltpu.VMEM((3, mine * nf // 2, half), F32),
            pltpu.VMEM((nf, 2 * mine, half), BF16),
            pltpu.VMEM((nf, 2 * mine, half), BF16),
            pltpu.SemaphoreType.DMA((6,)),
            pltpu.SemaphoreType.DMA((3,)),
            pltpu.SemaphoreType.DMA((2,)),
            pltpu.SemaphoreType.DMA((2,)),
            pltpu.SemaphoreType.DMA((2,)),
            pltpu.SemaphoreType.DMA((2,)),
            pltpu.SemaphoreType.DMA((2, 3, reach)),
            pltpu.SemaphoreType.DMA((2, 3, reach)),
            pltpu.SemaphoreType.DMA((ny,)),
            pltpu.SemaphoreType.DMA((ny,)),
            pltpu.SemaphoreType.REGULAR((nf,)),
        ],
        compiler_params=pltpu.CompilerParams(
            collective_id=0, has_side_effects=True, vmem_limit_bytes=53 * 1024 * 1024
        ),
        name="attention_backward",
    )(*flat, w_query[0], w_key[0], w_value[0], w_out[0])
    return sent.reshape(1, 1, per, places, chans), gvalue.T[None]


def solution(mesh):
    sizes = [mesh.shape[a] for a in ("frame", "dp", "pipe")]
    spread = P("pipe", "dp", "frame", None, None)
    return jax.shard_map(
        functools.partial(body, *sizes),
        mesh=mesh,
        in_specs=(spread, spread) + (P("pipe", None, None),) * 4,
        out_specs=(spread, P("pipe", None, ("frame", "dp"))),
        check_vma=False,
    )
```

```python
import functools

import jax
import jax.numpy as jnp
from jax import lax
from jax.experimental import pallas as pl
from jax.experimental.pallas import tpu as pltpu
from jax.sharding import PartitionSpec as P

HEADS = 12
HEAD_DIM = 64
PAIR = 2 * HEAD_DIM
PAIRS = HEADS // 2
SCALE = 0.125

BF16 = jnp.bfloat16
F32 = jnp.float32
MESH = pl.DeviceIdType.MESH

NN = (((1,), (0,)), ((), ()))
NT = (((1,), (1,)), ((), ()))
TN = (((0,), (0,)), ((), ()))


def dot(a, b, dims=NN):
    return lax.dot_general(a, b, dims, preferred_element_type=F32)


def wait_bytes(ref, sem):
    pltpu.make_async_copy(ref, ref, sem).wait()


def kernel(
    nf,
    ny,
    np_,
    acts,
    cot,
    w_query,
    w_key,
    w_value,
    w_out,
    sent,
    gvalue,
    acts_rx,
    proj_rx,
    proj_tx,
    acts_v,
    acts_tx,
    turn,
    cot_v,
    cot_rx,
    ret_tx,
    ret_rx,
    wq_v,
    wk_v,
    wv_v,
    wo_v,
    q_s,
    k_s,
    v_s,
    vg_s,
    dq_s,
    dk_s,
    order,
    vgt_b,
    prob,
    gv,
    rs_tx,
    rs_rx,
    fin_f,
    fin_tx,
    fin_rx,
    local_sem,
    acts_sem,
    proj_sem,
    cot_sem,
    ret_sem,
    fin_sem,
    rs_send,
    rs_recv,
    ready,
):
    me = lax.axis_index("frame")
    pipe = lax.axis_index("pipe")
    clip = lax.axis_index("dp")
    per = acts_rx.shape[1]
    chans = acts_rx.shape[2]
    inner = proj_rx.shape[2]
    rows = nf * per
    half = chans // 2
    reach = ny // 2
    messages = 2 * reach - 1
    mine = gvalue.shape[0]
    size = mine * nf

    loads = []
    for i, (src, dst) in enumerate(
        (
            (acts, acts_v),
            (cot, cot_v),
            (w_out, wo_v),
            (w_query, wq_v),
            (w_key, wk_v),
            (w_value, wv_v),
        )
    ):
        load = pltpu.make_async_copy(src, dst, local_sem.at[i])
        load.start()
        loads.append(load)

    barrier = pltpu.get_barrier_semaphore()
    up = lax.rem(clip + 1, ny)
    down = lax.rem(clip + ny - 1, ny)

    def greet(b, carry):
        pl.semaphore_signal(barrier, inc=1, device_id={"frame": b}, device_id_type=MESH)
        return carry

    lax.fori_loop(me + 1, nf, greet, 0)
    for y in (up, down):
        pl.semaphore_signal(barrier, inc=1, device_id={"dp": y}, device_id_type=MESH)
    pl.semaphore_signal(
        barrier, inc=1, device_id={"pipe": lax.rem(pipe + 1, np_)}, device_id_type=MESH
    )
    pl.semaphore_wait(barrier, me + 3)

    def answer(a, carry):
        pl.semaphore_signal(ready.at[me], inc=1, device_id={"frame": a}, device_id_type=MESH)
        return carry

    lax.fori_loop(0, me, answer, 0)

    def shift_of(i):
        near = lax.div(i, 2)
        odd = lax.rem(i, 2)
        return (near + 1) * (1 - odd) + (nf - 1 - near) * odd

    late = lax.div(2 * me, nf)

    def send(tx, rx, sends, recvs, to):
        pltpu.make_async_remote_copy(
            src_ref=tx.at[to],
            dst_ref=rx.at[me],
            send_sem=sends,
            recv_sem=recvs,
            device_id={"frame": to},
            device_id_type=MESH,
        ).start()

    def send_acts(to):
        send(acts_tx, acts_rx, acts_sem.at[2], acts_sem.at[late], to)

    def send_proj(to):
        send(proj_tx, proj_rx, proj_sem.at[0], proj_sem.at[1], to)

    def send_fin(to):
        send(fin_tx, fin_rx, fin_sem.at[0], fin_sem.at[1], to)

    def keep(tx, rx, sem):
        pltpu.make_async_copy(tx.at[me], rx.at[me], sem).start()

    def to_earlier(one):
        def step(i, carry):
            to = lax.rem(me + shift_of(nf - 2 - i), nf)
            pl.when(to < me)(lambda: one(to))
            return carry

        lax.fori_loop(0, nf - 1, step, 0)

    others = pl.ds(1, nf - 1)

    at = lax.broadcasted_iota(jnp.int32, (rows, rows), 0)
    column = lax.rem(at, per) * nf + lax.div(at, per)
    turn[...] = jnp.where(
        column == lax.broadcasted_iota(jnp.int32, (rows, rows), 1), 1.0, 0.0
    ).astype(BF16)
    loads[0].wait()
    acts_tx[...] = dot(turn[...], acts_v[...]).astype(BF16).reshape(nf, per, chans)
    keep(acts_tx, acts_rx, acts_sem.at[late])

    to_earlier(send_acts)

    loads[1].wait()
    loads[2].wait()
    projected = dot(cot_v[...], wo_v[...]).astype(BF16)
    proj_tx[...] = dot(turn[...], projected).astype(BF16).reshape(nf, per, inner)
    keep(proj_tx, proj_rx, proj_sem.at[1])
    to_earlier(send_proj)

    def to_later(to, carry):
        pl.semaphore_wait(ready.at[to], 1)
        send_acts(to)
        send_proj(to)
        return carry

    lax.fori_loop(me + 1, nf, to_later, 0)

    @pl.when(pipe > 0)
    def _():
        pltpu.make_async_remote_copy(
            src_ref=cot_v,
            dst_ref=cot_rx,
            send_sem=cot_sem.at[0],
            recv_sem=cot_sem.at[1],
            device_id={"pipe": pipe - 1},
            device_id_type=MESH,
        ).start()

    at = lax.broadcasted_iota(jnp.int32, (inner, inner), 0)
    column = lax.rem(lax.div(at, mine), nf) * (ny * mine) + lax.div(at, size) * mine + lax.rem(at, mine)
    order[...] = jnp.where(
        column == lax.broadcasted_iota(jnp.int32, (inner, inner), 1), 1.0, 0.0
    ).astype(BF16)

    wait_bytes(acts_rx.at[others], acts_sem.at[2])
    wait_bytes(proj_rx.at[others], proj_sem.at[0])

    for load in loads[3:]:
        load.wait()
    few = nf // 2
    for e in range(2):
        slots = pl.ds(e * few, few)
        block = pl.ds(e * few * per, few * per)
        wait_bytes(acts_rx.at[slots], acts_sem.at[e])
        inputs = acts_rx[slots].reshape(few * per, chans)
        q_s[block, :] = dot(inputs, wq_v[...]).astype(BF16)
        k_s[block, :] = dot(inputs, wk_v[...]).astype(BF16)
    inputs = acts_rx[...].reshape(rows, chans)
    wait_bytes(proj_rx, proj_sem.at[1])
    lane = lax.broadcasted_iota(jnp.int32, (1, PAIR), 1)
    masks = [jnp.where(lane // HEAD_DIM == e, 1.0, 0.0).astype(BF16) for e in range(2)]

    for pair in range(PAIRS):
        cols = pl.ds(pair * PAIR, PAIR)
        q = q_s[:, cols]
        k = k_s[:, cols]
        p = proj_rx[:, :, cols].reshape(rows, PAIR)
        total = jnp.zeros((rows, PAIR), F32)
        for e in range(2):
            scores = dot(k * masks[e], q, NT) * SCALE
            scores = jnp.exp(scores - jnp.max(scores, axis=0, keepdims=True))
            scores = scores * (1.0 / jnp.sum(scores, axis=0, keepdims=True))
            prob[2 * pair + e] = scores
            total = total + dot(scores.astype(BF16), p * masks[e])
        vg_s[:, cols] = total.astype(BF16)

    vgt_b[...] = dot(order[...], vg_s[...], NT).astype(BF16)

    def sum_for(away):
        o = lax.rem(clip + away, ny)
        at = pl.ds(pl.multiple_of(o * size, size), size)
        gv[o] = dot(vgt_b[at, :], inputs)

    def own(o, h):
        return gv[o, :, h * half : (h + 1) * half]

    def ring(d, j):
        return pltpu.make_async_remote_copy(
            src_ref=rs_tx.at[d, j],
            dst_ref=rs_rx.at[d, j],
            send_sem=rs_send.at[d, j],
            recv_sem=rs_recv.at[d, j],
            device_id={"dp": (up, down)[d]},
            device_id_type=MESH,
        )

    def ring_step(j):
        away = reach - (j + 1) // 2
        for d in range(2):
            h = (j + d) % 2
            o = lax.rem(clip + (away if d == 0 else ny - away), ny)
            value = own(o, h)
            if j >= 2:
                ring(d, j - 2).wait_recv()
                value = value + rs_rx[d, j - 2].astype(F32)
            rs_tx[d, j] = value.astype(BF16)
            ring(d, j).start()

    sum_for(reach)
    ring_step(0)
    if messages > 1:
        sum_for(reach - 1)
        sum_for(ny - reach + 1)
        ring_step(1)
    for away in range(reach - 1):
        sum_for(away)
        if away:
            sum_for(ny - away)
    if messages == 1:
        sum_for(0)

    v_s[...] = dot(inputs, wv_v[...]).astype(BF16)
    for pair in range(PAIRS):
        cols = pl.ds(pair * PAIR, PAIR)
        q = q_s[:, cols]
        k = k_s[:, cols]
        v = v_s[:, cols]
        p = proj_rx[:, :, cols].reshape(rows, PAIR)
        dq = jnp.zeros((rows, PAIR), F32)
        dk = jnp.zeros((rows, PAIR), F32)
        for e in range(2):
            probability = prob[2 * pair + e]
            grad = dot(v * masks[e], p, NT)
            mean = jnp.sum(grad * probability, axis=0, keepdims=True)
            grad = (probability * (grad - mean)).astype(BF16)
            dk = dk + dot(grad, q * masks[e])
            dq = dq + dot(grad, k * masks[e], TN)
        dq_s[:, cols] = (dq * SCALE).astype(BF16)
        dk_s[:, cols] = (dk * SCALE).astype(BF16)

    @pl.when(pipe > 0)
    def _():
        branch = dot(dq_s[...], wq_v[...], NT)
        branch = branch + dot(dk_s[...], wk_v[...], NT)
        branch = branch + dot(vg_s[...], wv_v[...], NT)
        ret_tx[...] = branch.astype(BF16).reshape(nf, per, chans)

        def one(i, carry):
            to = lax.rem(me + shift_of(i) * jnp.minimum(nf - 1 - i, 1), nf)
            pltpu.make_async_remote_copy(
                src_ref=ret_tx.at[to],
                dst_ref=ret_rx.at[me],
                send_sem=ret_sem.at[0],
                recv_sem=ret_sem.at[1],
                device_id={"frame": to, "pipe": pipe - 1},
                device_id_type=MESH,
            ).start()
            return carry

        lax.fori_loop(0, nf, one, 0)

    for j in range(2, messages):
        ring_step(j)

    for d in range(2):
        for j in range(max(0, messages - 2), messages):
            ring(d, j).wait_recv()
    for h in range(2):
        value = own(clip, h)
        for d in range(2):
            j = messages - 1 - (h + d) % 2
            if j >= 0:
                value = value + rs_rx[d, j].astype(F32)
        fin_f[h] = value
    for f in range(nf):
        at = slice(f * mine, (f + 1) * mine)
        fin_tx[f] = jnp.concatenate([fin_f[0, at, :], fin_f[1, at, :]], axis=0).astype(BF16)
    keep(fin_tx, fin_rx, fin_sem.at[1])

    def finish(i, carry):
        send_fin(lax.rem(me + shift_of(i), nf))
        return carry

    lax.fori_loop(0, nf - 1, finish, 0)

    @pl.when(pipe < np_ - 1)
    def _():
        wait_bytes(cot_rx, cot_sem.at[1])
        wait_bytes(ret_rx, ret_sem.at[1])
        branch = dot(turn[...], ret_rx[...].reshape(rows, chans), TN)
        sent[...] = (cot_rx[...].astype(F32) + branch).astype(BF16)

    @pl.when(pipe == np_ - 1)
    def _():
        sent[...] = jnp.zeros_like(sent)

    wait_bytes(fin_rx, fin_sem.at[1])
    total = jnp.sum(fin_rx[...].astype(F32), axis=0)
    for h in range(2):
        gvalue[:, h * half : (h + 1) * half] = total[h * mine : (h + 1) * mine]

    wait_bytes(fin_rx.at[others], fin_sem.at[0])
    for d in range(2):
        for j in range(messages):
            ring(d, j).wait_send()

    @pl.when(pipe > 0)
    def _():
        wait_bytes(cot_rx, cot_sem.at[0])
        wait_bytes(ret_rx, ret_sem.at[0])


def body(nf, ny, np_, acts, cotangent, w_query, w_key, w_value, w_out):
    per, places, chans = acts.shape[2:]
    inner = w_out.shape[2]
    rows = nf * per
    mine = inner // (nf * ny)
    messages = 2 * (ny // 2) - 1
    half = chans // 2
    flat = [a[0, 0].reshape(per * places, chans) for a in (acts, cotangent)]
    anywhere = pl.BlockSpec(memory_space=pl.ANY)
    in_vmem = pl.BlockSpec(memory_space=pltpu.VMEM)
    sent, gvalue = pl.pallas_call(
        functools.partial(kernel, nf, ny, np_),
        out_shape=(
            jax.ShapeDtypeStruct((rows, chans), BF16),
            jax.ShapeDtypeStruct((mine, chans), F32),
        ),
        in_specs=[anywhere] * 6,
        out_specs=(in_vmem, in_vmem),
        scratch_shapes=[
            pltpu.VMEM((nf, per, chans), BF16),
            pltpu.VMEM((nf, per, inner), BF16),
            pltpu.VMEM((nf, per, inner), BF16),
            pltpu.VMEM((rows, chans), BF16),
            pltpu.VMEM((nf, per, chans), BF16),
            pltpu.VMEM((rows, rows), BF16),
            pltpu.VMEM((rows, chans), BF16),
            pltpu.VMEM((rows, chans), BF16),
            pltpu.VMEM((nf, per, chans), BF16),
            pltpu.VMEM((nf, per, chans), BF16),
            pltpu.VMEM((chans, inner), BF16),
            pltpu.VMEM((chans, inner), BF16),
            pltpu.VMEM((chans, inner), BF16),
            pltpu.VMEM((chans, inner), BF16),
            pltpu.VMEM((rows, inner), BF16),
            pltpu.VMEM((rows, inner), BF16),
            pltpu.VMEM((rows, inner), BF16),
            pltpu.VMEM((rows, inner), BF16),
            pltpu.VMEM((rows, inner), BF16),
            pltpu.VMEM((rows, inner), BF16),
            pltpu.VMEM((inner, inner), BF16),
            pltpu.VMEM((inner, rows), BF16),
            pltpu.VMEM((HEADS, rows, rows), F32),
            pltpu.VMEM((ny, mine * nf, chans), F32),
            pltpu.VMEM((2, messages, mine * nf, half), BF16),
            pltpu.VMEM((2, messages, mine * nf, half), BF16),
            pltpu.VMEM((2, mine * nf, half), F32),
            pltpu.VMEM((nf, 2 * mine, half), BF16),
            pltpu.VMEM((nf, 2 * mine, half), BF16),
            pltpu.SemaphoreType.DMA((6,)),
            pltpu.SemaphoreType.DMA((3,)),
            pltpu.SemaphoreType.DMA((2,)),
            pltpu.SemaphoreType.DMA((2,)),
            pltpu.SemaphoreType.DMA((2,)),
            pltpu.SemaphoreType.DMA((2,)),
            pltpu.SemaphoreType.DMA((2, messages)),
            pltpu.SemaphoreType.DMA((2, messages)),
            pltpu.SemaphoreType.REGULAR((nf,)),
        ],
        compiler_params=pltpu.CompilerParams(
            collective_id=0, has_side_effects=True, vmem_limit_bytes=53 * 1024 * 1024
        ),
        name="attention_backward",
    )(*flat, w_query[0], w_key[0], w_value[0], w_out[0])
    return sent.reshape(1, 1, per, places, chans), gvalue.T[None]


def solution(mesh):
    sizes = [mesh.shape[a] for a in ("frame", "dp", "pipe")]
    spread = P("pipe", "dp", "frame", None, None)
    return jax.shard_map(
        functools.partial(body, *sizes),
        mesh=mesh,
        in_specs=(spread, spread) + (P("pipe", None, None),) * 4,
        out_specs=(spread, P("pipe", None, ("frame", "dp"))),
        check_vma=False,
    )
```

```python
import functools

import jax
import jax.numpy as jnp
from jax import lax
from jax.experimental import pallas as pl
from jax.experimental.pallas import tpu as pltpu
from jax.sharding import PartitionSpec as P

HEADS = 12
HEAD_DIM = 64
PAIR = 2 * HEAD_DIM
PAIRS = HEADS // 2
SCALE = 0.125

BF16 = jnp.bfloat16
F32 = jnp.float32
MESH = pl.DeviceIdType.MESH

NN = (((1,), (0,)), ((), ()))
NT = (((1,), (1,)), ((), ()))
TN = (((0,), (0,)), ((), ()))


def dot(a, b, dims=NN):
    return lax.dot_general(a, b, dims, preferred_element_type=F32)


def wait_bytes(ref, sem):
    pltpu.make_async_copy(ref, ref, sem).wait()


def kernel(
    nf,
    ny,
    np_,
    acts,
    cot,
    w_query,
    w_key,
    w_value,
    w_out,
    sent,
    gvalue,
    acts_rx,
    proj_rx,
    proj_tx,
    acts_v,
    acts_tx,
    turn,
    cot_v,
    cot_rx,
    ret_tx,
    ret_rx,
    wq_v,
    wk_v,
    wv_v,
    wo_v,
    q_s,
    k_s,
    v_s,
    vg_s,
    dq_s,
    dk_s,
    order,
    vgt_b,
    prob,
    gv,
    rs_tx,
    rs_rx,
    fin_f,
    fin_tx,
    fin_rx,
    local_sem,
    acts_sem,
    proj_sem,
    cot_sem,
    ret_sem,
    fin_sem,
    rs_send,
    rs_recv,
    ready,
):
    me = lax.axis_index("frame")
    pipe = lax.axis_index("pipe")
    clip = lax.axis_index("dp")
    per = acts_rx.shape[1]
    chans = acts_rx.shape[2]
    inner = proj_rx.shape[2]
    rows = nf * per
    half = chans // 2
    reach = ny // 2
    messages = 2 * reach - 1
    mine = gvalue.shape[0]
    size = mine * nf

    loads = []
    for i, (src, dst) in enumerate(
        (
            (acts, acts_v),
            (cot, cot_v),
            (w_out, wo_v),
            (w_query, wq_v),
            (w_key, wk_v),
            (w_value, wv_v),
        )
    ):
        load = pltpu.make_async_copy(src, dst, local_sem.at[i])
        load.start()
        loads.append(load)

    barrier = pltpu.get_barrier_semaphore()
    up = lax.rem(clip + 1, ny)
    down = lax.rem(clip + ny - 1, ny)

    def greet(b, carry):
        pl.semaphore_signal(barrier, inc=1, device_id={"frame": b}, device_id_type=MESH)
        return carry

    lax.fori_loop(me + 1, nf, greet, 0)
    for y in (up, down):
        pl.semaphore_signal(barrier, inc=1, device_id={"dp": y}, device_id_type=MESH)
    pl.semaphore_signal(
        barrier, inc=1, device_id={"pipe": lax.rem(pipe + 1, np_)}, device_id_type=MESH
    )
    pl.semaphore_wait(barrier, me + 3)

    def answer(a, carry):
        pl.semaphore_signal(ready.at[me], inc=1, device_id={"frame": a}, device_id_type=MESH)
        return carry

    lax.fori_loop(0, me, answer, 0)

    def shift_of(i):
        near = lax.div(i, 2)
        odd = lax.rem(i, 2)
        return (near + 1) * (1 - odd) + (nf - 1 - near) * odd

    late = lax.div(2 * me, nf)

    def send(tx, rx, sends, recvs, to):
        pltpu.make_async_remote_copy(
            src_ref=tx.at[to],
            dst_ref=rx.at[me],
            send_sem=sends,
            recv_sem=recvs,
            device_id={"frame": to},
            device_id_type=MESH,
        ).start()

    def send_acts(to):
        send(acts_tx, acts_rx, acts_sem.at[2], acts_sem.at[late], to)

    def send_proj(to):
        send(proj_tx, proj_rx, proj_sem.at[0], proj_sem.at[1], to)

    def send_fin(to):
        send(fin_tx, fin_rx, fin_sem.at[0], fin_sem.at[1], to)

    def keep(tx, rx, sem):
        pltpu.make_async_copy(tx.at[me], rx.at[me], sem).start()

    def to_earlier(one):
        def step(i, carry):
            to = lax.rem(me + shift_of(nf - 2 - i), nf)
            pl.when(to < me)(lambda: one(to))
            return carry

        lax.fori_loop(0, nf - 1, step, 0)

    others = pl.ds(1, nf - 1)

    at = lax.broadcasted_iota(jnp.int32, (rows, rows), 0)
    column = lax.rem(at, per) * nf + lax.div(at, per)
    turn[...] = jnp.where(
        column == lax.broadcasted_iota(jnp.int32, (rows, rows), 1), 1.0, 0.0
    ).astype(BF16)
    loads[0].wait()
    acts_tx[...] = dot(turn[...], acts_v[...]).astype(BF16).reshape(nf, per, chans)
    keep(acts_tx, acts_rx, acts_sem.at[late])

    to_earlier(send_acts)

    loads[1].wait()
    loads[2].wait()
    projected = dot(cot_v[...], wo_v[...]).astype(BF16)
    proj_tx[...] = dot(turn[...], projected).astype(BF16).reshape(nf, per, inner)
    keep(proj_tx, proj_rx, proj_sem.at[1])
    to_earlier(send_proj)

    def to_later(to, carry):
        pl.semaphore_wait(ready.at[to], 1)
        send_acts(to)
        send_proj(to)
        return carry

    lax.fori_loop(me + 1, nf, to_later, 0)

    @pl.when(pipe > 0)
    def _():
        pltpu.make_async_remote_copy(
            src_ref=cot_v,
            dst_ref=cot_rx,
            send_sem=cot_sem.at[0],
            recv_sem=cot_sem.at[1],
            device_id={"pipe": pipe - 1},
            device_id_type=MESH,
        ).start()

    at = lax.broadcasted_iota(jnp.int32, (inner, inner), 0)
    column = lax.rem(lax.div(at, mine), nf) * (ny * mine) + lax.div(at, size) * mine + lax.rem(at, mine)
    order[...] = jnp.where(
        column == lax.broadcasted_iota(jnp.int32, (inner, inner), 1), 1.0, 0.0
    ).astype(BF16)

    wait_bytes(acts_rx.at[others], acts_sem.at[2])
    wait_bytes(proj_rx.at[others], proj_sem.at[0])

    for load in loads[3:]:
        load.wait()
    few = nf // 2
    for e in range(2):
        slots = pl.ds(e * few, few)
        block = pl.ds(e * few * per, few * per)
        wait_bytes(acts_rx.at[slots], acts_sem.at[e])
        inputs = acts_rx[slots].reshape(few * per, chans)
        q_s[block, :] = dot(inputs, wq_v[...]).astype(BF16)
        k_s[block, :] = dot(inputs, wk_v[...]).astype(BF16)
    inputs = acts_rx[...].reshape(rows, chans)
    wait_bytes(proj_rx, proj_sem.at[1])
    lane = lax.broadcasted_iota(jnp.int32, (1, PAIR), 1)
    masks = [jnp.where(lane // HEAD_DIM == e, 1.0, 0.0).astype(BF16) for e in range(2)]

    for pair in range(PAIRS):
        cols = pl.ds(pair * PAIR, PAIR)
        q = q_s[:, cols]
        k = k_s[:, cols]
        p = proj_rx[:, :, cols].reshape(rows, PAIR)
        total = jnp.zeros((rows, PAIR), F32)
        for e in range(2):
            scores = dot(k * masks[e], q, NT) * SCALE
            scores = jnp.exp(scores - jnp.max(scores, axis=0, keepdims=True))
            scores = scores * (1.0 / jnp.sum(scores, axis=0, keepdims=True))
            prob[2 * pair + e] = scores
            total = total + dot(scores.astype(BF16), p * masks[e])
        vg_s[:, cols] = total.astype(BF16)

    vgt_b[...] = dot(order[...], vg_s[...], NT).astype(BF16)

    def sum_for(away):
        o = lax.rem(clip + away, ny)
        at = pl.ds(pl.multiple_of(o * size, size), size)
        gv[o] = dot(vgt_b[at, :], inputs)

    def own(o, h):
        return gv[o, :, h * half : (h + 1) * half]

    def ring(d, j):
        return pltpu.make_async_remote_copy(
            src_ref=rs_tx.at[d, j],
            dst_ref=rs_rx.at[d, j],
            send_sem=rs_send.at[d, j],
            recv_sem=rs_recv.at[d, j],
            device_id={"dp": (up, down)[d]},
            device_id_type=MESH,
        )

    def ring_step(j):
        away = reach - (j + 1) // 2
        for d in range(2):
            h = (j + d) % 2
            o = lax.rem(clip + (away if d == 0 else ny - away), ny)
            value = own(o, h)
            if j >= 2:
                ring(d, j - 2).wait_recv()
                value = value + rs_rx[d, j - 2].astype(F32)
            rs_tx[d, j] = value.astype(BF16)
            ring(d, j).start()

    sum_for(reach)
    ring_step(0)
    if messages > 1:
        sum_for(reach - 1)
        sum_for(ny - reach + 1)
        ring_step(1)
    for away in range(reach - 1):
        sum_for(away)
        if away:
            sum_for(ny - away)
    if messages == 1:
        sum_for(0)

    v_s[...] = dot(inputs, wv_v[...]).astype(BF16)
    for pair in range(PAIRS):
        cols = pl.ds(pair * PAIR, PAIR)
        q = q_s[:, cols]
        k = k_s[:, cols]
        v = v_s[:, cols]
        p = proj_rx[:, :, cols].reshape(rows, PAIR)
        dq = jnp.zeros((rows, PAIR), F32)
        dk = jnp.zeros((rows, PAIR), F32)
        for e in range(2):
            probability = prob[2 * pair + e]
            grad = dot(v * masks[e], p, NT)
            mean = jnp.sum(grad * probability, axis=0, keepdims=True)
            grad = (probability * (grad - mean)).astype(BF16)
            dk = dk + dot(grad, q * masks[e])
            dq = dq + dot(grad, k * masks[e], TN)
        dq_s[:, cols] = (dq * SCALE).astype(BF16)
        dk_s[:, cols] = (dk * SCALE).astype(BF16)

    @pl.when(pipe > 0)
    def _():
        branch = dot(dq_s[...], wq_v[...], NT)
        branch = branch + dot(dk_s[...], wk_v[...], NT)
        branch = branch + dot(vg_s[...], wv_v[...], NT)
        ret_tx[...] = branch.astype(BF16).reshape(nf, per, chans)

    def give_back(i, carry):
        to = lax.rem(me + shift_of(i) * jnp.minimum(nf - 1 - i, 1), nf)
        pltpu.make_async_remote_copy(
            src_ref=ret_tx.at[to],
            dst_ref=ret_rx.at[me],
            send_sem=ret_sem.at[0],
            recv_sem=ret_sem.at[1],
            device_id={"frame": to, "pipe": pipe - 1},
            device_id_type=MESH,
        ).start()
        return carry

    def give_back_some(first, last):
        @pl.when(pipe > 0)
        def _():
            lax.fori_loop(first, last, give_back, 0)

    few = -(-nf // 3)
    give_back_some(0, few)
    for j in range(2, max(messages, 3 + 1)):
        if j < messages:
            ring_step(j)
        if j <= 3:
            give_back_some((j - 1) * few, min((j) * few, nf))

    for d in range(2):
        for j in range(max(0, messages - 2), messages):
            ring(d, j).wait_recv()
    for h in range(2):
        value = own(clip, h)
        for d in range(2):
            j = messages - 1 - (h + d) % 2
            if j >= 0:
                value = value + rs_rx[d, j].astype(F32)
        fin_f[h] = value
    for f in range(nf):
        at = slice(f * mine, (f + 1) * mine)
        fin_tx[f] = jnp.concatenate([fin_f[0, at, :], fin_f[1, at, :]], axis=0).astype(BF16)
    keep(fin_tx, fin_rx, fin_sem.at[1])

    def finish(i, carry):
        send_fin(lax.rem(me + shift_of(i), nf))
        return carry

    lax.fori_loop(0, nf - 1, finish, 0)

    @pl.when(pipe < np_ - 1)
    def _():
        wait_bytes(cot_rx, cot_sem.at[1])
        wait_bytes(ret_rx, ret_sem.at[1])
        branch = dot(turn[...], ret_rx[...].reshape(rows, chans), TN)
        sent[...] = (cot_rx[...].astype(F32) + branch).astype(BF16)

    @pl.when(pipe == np_ - 1)
    def _():
        sent[...] = jnp.zeros_like(sent)

    wait_bytes(fin_rx, fin_sem.at[1])
    total = jnp.sum(fin_rx[...].astype(F32), axis=0)
    for h in range(2):
        gvalue[:, h * half : (h + 1) * half] = total[h * mine : (h + 1) * mine]

    wait_bytes(fin_rx.at[others], fin_sem.at[0])
    for d in range(2):
        for j in range(messages):
            ring(d, j).wait_send()

    @pl.when(pipe > 0)
    def _():
        wait_bytes(cot_rx, cot_sem.at[0])
        wait_bytes(ret_rx, ret_sem.at[0])


def body(nf, ny, np_, acts, cotangent, w_query, w_key, w_value, w_out):
    per, places, chans = acts.shape[2:]
    inner = w_out.shape[2]
    rows = nf * per
    mine = inner // (nf * ny)
    messages = 2 * (ny // 2) - 1
    half = chans // 2
    flat = [a[0, 0].reshape(per * places, chans) for a in (acts, cotangent)]
    anywhere = pl.BlockSpec(memory_space=pl.ANY)
    in_vmem = pl.BlockSpec(memory_space=pltpu.VMEM)
    sent, gvalue = pl.pallas_call(
        functools.partial(kernel, nf, ny, np_),
        out_shape=(
            jax.ShapeDtypeStruct((rows, chans), BF16),
            jax.ShapeDtypeStruct((mine, chans), F32),
        ),
        in_specs=[anywhere] * 6,
        out_specs=(in_vmem, in_vmem),
        scratch_shapes=[
            pltpu.VMEM((nf, per, chans), BF16),
            pltpu.VMEM((nf, per, inner), BF16),
            pltpu.VMEM((nf, per, inner), BF16),
            pltpu.VMEM((rows, chans), BF16),
            pltpu.VMEM((nf, per, chans), BF16),
            pltpu.VMEM((rows, rows), BF16),
            pltpu.VMEM((rows, chans), BF16),
            pltpu.VMEM((rows, chans), BF16),
            pltpu.VMEM((nf, per, chans), BF16),
            pltpu.VMEM((nf, per, chans), BF16),
            pltpu.VMEM((chans, inner), BF16),
            pltpu.VMEM((chans, inner), BF16),
            pltpu.VMEM((chans, inner), BF16),
            pltpu.VMEM((chans, inner), BF16),
            pltpu.VMEM((rows, inner), BF16),
            pltpu.VMEM((rows, inner), BF16),
            pltpu.VMEM((rows, inner), BF16),
            pltpu.VMEM((rows, inner), BF16),
            pltpu.VMEM((rows, inner), BF16),
            pltpu.VMEM((rows, inner), BF16),
            pltpu.VMEM((inner, inner), BF16),
            pltpu.VMEM((inner, rows), BF16),
            pltpu.VMEM((HEADS, rows, rows), F32),
            pltpu.VMEM((ny, mine * nf, chans), F32),
            pltpu.VMEM((2, messages, mine * nf, half), BF16),
            pltpu.VMEM((2, messages, mine * nf, half), BF16),
            pltpu.VMEM((2, mine * nf, half), F32),
            pltpu.VMEM((nf, 2 * mine, half), BF16),
            pltpu.VMEM((nf, 2 * mine, half), BF16),
            pltpu.SemaphoreType.DMA((6,)),
            pltpu.SemaphoreType.DMA((3,)),
            pltpu.SemaphoreType.DMA((2,)),
            pltpu.SemaphoreType.DMA((2,)),
            pltpu.SemaphoreType.DMA((2,)),
            pltpu.SemaphoreType.DMA((2,)),
            pltpu.SemaphoreType.DMA((2, messages)),
            pltpu.SemaphoreType.DMA((2, messages)),
            pltpu.SemaphoreType.REGULAR((nf,)),
        ],
        compiler_params=pltpu.CompilerParams(
            collective_id=0, has_side_effects=True, vmem_limit_bytes=53 * 1024 * 1024
        ),
        name="attention_backward",
    )(*flat, w_query[0], w_key[0], w_value[0], w_out[0])
    return sent.reshape(1, 1, per, places, chans), gvalue.T[None]


def solution(mesh):
    sizes = [mesh.shape[a] for a in ("frame", "dp", "pipe")]
    spread = P("pipe", "dp", "frame", None, None)
    return jax.shard_map(
        functools.partial(body, *sizes),
        mesh=mesh,
        in_specs=(spread, spread) + (P("pipe", None, None),) * 4,
        out_specs=(spread, P("pipe", None, ("frame", "dp"))),
        check_vma=False,
    )
```
